32 devices in a mesh: grp: 2 (over y), tr: 8 (over z, x), root: 2 (over core).
Axes of the slice: x: 2, y: 2, z: 4, core: 2. Of those that a mesh axis runs over, the one named last changes fastest.
Arguments:
- residual: bfloat16 [128, 65536], P('root', ('grp', 'tr')), parts along dimension 1, may hold values from -8 to 8
- subspace: bfloat16 [512, 65536], P(None, ('grp', 'tr')), parts along dimension 1, may hold values from -1 to 1, as said below
- inverses: bfloat16 [16, 512, 512], P(('grp', 'tr')), parts along dimension 0, may hold values from -1 to 3, as said below
- owner_offset: int32 [128], P(('grp', 'tr')), parts along dimension 0, may hold values from 0 to 3, as said below
- listed: int32 [128], P(('grp', 'tr')), parts along dimension 0, may hold values from 0 to 1, as said below
Outputs:
- corrections: float32 [128, 65536], P('root', ('grp', 'tr')), parts along dimension 1
The draws below stay inside these ranges and needn't reach their ends.
There are 2 independent parts, one for each index of `grp`. The reference program is written for one: setup_inputs(seed, part) draws one part's arguments, and reference() takes and returns one part's arrays. A program takes and returns all parts, laid end to end along the dimension named above; each array names one. Nothing has to cross between parts.
Inputs may be any that keep to these rules, and one draw needn't show every extreme that they name: Each entry of subspace lies within the stated range; rows are not normalized. `inverses`: each inverse is a dense real matrix. `owner_offset`: among the 8 blocks of each shard, at least one is listed and has offset 3. Each shard has at least one listed block and at least one unlisted block.
All inputs are finite; a program needn't handle non-finite values.
Results may differ from the reference program's by a relative error of at most 0.0065.
Values may be sent and summed in bfloat16 or wider, within the bound.
No kernel may reach another device: no remote copies, remote signals or barrier semaphores. Data moves between devices by JAX's collectives and lax.ppermute only.
A program may use at most 64 MiB of HBM per device.

```python
import math
import jax
import jax.numpy as jnp
from jax import lax

BLK = 512
R = 128
S = 512
OFFS = 4
PASSES = 2
BLK_DEV = 8
NB = 64
NT = 32768
PAIRS = 8


def subspace_values(key):
    base = jax.random.fold_in(key, 11)
    row_key, common_key, mix_key, scale_key = jax.random.split(base, 4)
    position = jnp.arange(NT, dtype=jnp.float32) / NT
    rows = jax.random.truncated_normal(row_key, -4.0, 4.0, (S, NT), jnp.float32)
    common = jax.random.truncated_normal(common_key, -4.0, 4.0, (8, NT), jnp.float32)
    mixing = jax.random.truncated_normal(mix_key, -4.0, 4.0, (S, 8), jnp.float32) * math.sqrt(0.6 / S)
    scales = jnp.exp(jax.random.uniform(scale_key, (S,), jnp.float32, math.log(0.6), math.log(1.25)))
    envelope = jnp.exp(0.5 * math.log(3.0) * position)
    envelope = envelope / jnp.sqrt(jnp.mean(envelope * envelope))
    entries = rows + jnp.dot(mixing, common, precision=lax.Precision.HIGHEST)
    return entries * envelope[None, :] * scales[:, None] / jnp.sqrt(jnp.float32(NT))


def draw_subspace(key, part):
    return subspace_values(key).astype(jnp.bfloat16)


def draw_residual(key, part):
    basis = subspace_values(key)
    noise_key, weight_key = jax.random.split(jax.random.fold_in(key, 37))
    noise = jax.random.truncated_normal(noise_key, -4.0, 4.0, (R, NT), jnp.float32)
    weights = jax.random.truncated_normal(weight_key, -4.0, 4.0, (R, S), jnp.float32)
    row_norms = jnp.sqrt(jnp.sum(basis * basis, axis=1))
    weights = weights * jnp.sqrt(jnp.float32(NT) / S) / row_norms[None, :]
    values = noise + jnp.dot(weights, basis, precision=lax.Precision.HIGHEST)
    return jnp.clip(values, -8.0, 8.0).astype(jnp.bfloat16)


def draw_inverses(key, part):
    first_key, second_key = jax.random.split(jax.random.fold_in(key, 23))
    diagonal = jnp.exp(jax.random.uniform(first_key, (PAIRS, BLK), jnp.float32, math.log(0.5), math.log(2.0)))
    off_diagonal = jax.random.truncated_normal(second_key, -4.0, 4.0, (PAIRS, BLK, BLK), jnp.float32) * (0.5 / math.sqrt(BLK))
    matrix = off_diagonal + jnp.eye(BLK, dtype=jnp.float32)[None, :, :] * diagonal[:, None, :]
    return matrix.astype(jnp.bfloat16)


def block_plan(key):
    plan_key = jax.random.fold_in(key, 71)
    offset_key, listed_key, forced_key = jax.random.split(plan_key, 3)
    shard_count = NB // BLK_DEV
    offsets = jax.random.randint(offset_key, (NB,), 0, OFFS, dtype=jnp.int32)
    marks = (jax.random.randint(listed_key, (NB,), 0, 8, dtype=jnp.int32) < 7).astype(jnp.int32)
    forced_slot = jax.random.randint(forced_key, (shard_count,), 0, BLK_DEV, dtype=jnp.int32)
    skipped_slot = (forced_slot + 1) % BLK_DEV
    within = jnp.arange(NB, dtype=jnp.int32) % BLK_DEV
    forced = within == jnp.repeat(forced_slot, BLK_DEV)
    skipped = within == jnp.repeat(skipped_slot, BLK_DEV)
    offsets = jnp.where(forced, OFFS - 1, offsets).astype(jnp.int32)
    marks = jnp.where(skipped, 0, marks).astype(jnp.int32)
    marks = jnp.where(forced, 1, marks).astype(jnp.int32)
    return (offsets, marks)


def draw_owner_offset(key, part):
    return block_plan(key)[0]


def draw_listed(key, part):
    return block_plan(key)[1]


def setup_inputs(seed: int = 0, part: int = 0) -> dict:
    splits = jax.random.split(jax.random.key(seed), 6)
    part_keys = jax.random.split(jax.random.fold_in(splits[5], part), 6)
    return {
        "residual": draw_residual(jax.random.fold_in(jax.random.fold_in(splits[5], part), 71), part),
        "subspace": draw_subspace(jax.random.fold_in(jax.random.fold_in(splits[5], part), 71), part),
        "inverses": draw_inverses(jax.random.fold_in(jax.random.fold_in(splits[5], part), 71), part),
        "owner_offset": draw_owner_offset(jax.random.fold_in(jax.random.fold_in(splits[5], part), 71), part),
        "listed": draw_listed(jax.random.fold_in(jax.random.fold_in(splits[5], part), 71), part),
    }


def reference(residual, subspace, inverses, owner_offset, listed):
    block_count = residual.shape[1] // BLK
    blocks = residual.reshape(R, block_count, BLK).transpose(1, 0, 2)
    holder = jnp.arange(block_count, dtype=jnp.int32) // BLK_DEV
    owner_pair = ((holder + owner_offset) % PAIRS).astype(jnp.int32)

    def apply_block(packet):
        residual_block, pair_index, is_listed = packet
        solved = jnp.dot(residual_block, inverses[pair_index], preferred_element_type=jnp.float32)
        return jnp.where(is_listed > 0, solved, residual_block.astype(jnp.float32))

    precond = lax.map(apply_block, (blocks, owner_pair, listed))
    current = precond.transpose(1, 0, 2).reshape(R, block_count * BLK)
    for repeat in range(PASSES):
        rounded = current.astype(jnp.bfloat16)
        correlation = lax.dot_general(rounded, subspace, (((1,), (1,)), ((), ())), preferred_element_type=jnp.float32)
        coefficients = correlation.astype(jnp.bfloat16)
        current = current - jnp.dot(coefficients, subspace, preferred_element_type=jnp.float32)
    return current
```

```python
import jax
import jax.numpy as jnp
from jax import lax
from jax.experimental import pallas as pl
from jax.experimental.pallas import tpu as pltpu
from jax.sharding import PartitionSpec as P

OFFS = 4
F32 = jnp.float32
BF16 = jnp.bfloat16
VMEM = pl.BlockSpec(memory_space=pltpu.VMEM)
SMEM = pl.BlockSpec(memory_space=pltpu.SMEM)
ACROSS = (((1,), (1,)), ((), ()))


def from_ahead(block, distance):
    n = lax.axis_size("tr")
    return lax.ppermute(block, "tr", [((i + distance) % n, i) for i in range(n)])


def other_core(block):
    return lax.ppermute(block, "root", [(0, 1), (1, 0)])


def sum_over_tr(part):
    n = lax.axis_size("tr")
    step = 1
    while step < n:
        part = part + lax.ppermute(part, "tr", [(i, i ^ step) for i in range(n)])
        step *= 2
    return part


def precond_kernel(
    offset_ref, listed_ref, core_ref, residual_ref, subspace_ref, own_ref,
    *rest,
):
    halves, (precond_ref, corr_ref, total_ref) = rest[:-3], rest[-3:]
    size = own_ref.shape[0]
    half = halves[0].shape[0]
    mine = core_ref[0] * half
    total_ref[...] = jnp.zeros_like(total_ref)

    @pl.loop(0, residual_ref.shape[1] // size)
    def _(b):
        base = b * size
        columns = pl.ds(pl.multiple_of(base, size), size)
        of_mine = pl.ds(pl.multiple_of(base + mine, half), half)
        of_other = pl.ds(pl.multiple_of(base + half - mine, half), half)
        marked = listed_ref[b] > 0
        offset = offset_ref[b]

        @pl.when(jnp.logical_not(marked))
        def _():
            precond_ref[:, columns] = residual_ref[:, columns].astype(F32)

        @pl.when(jnp.logical_and(marked, offset == 0))
        def _():
            precond_ref[:, columns] = jnp.dot(
                residual_ref[:, columns], own_ref[...], preferred_element_type=F32
            )

        for distance in range(1, OFFS):
            @pl.when(jnp.logical_and(marked, offset == distance))
            def _():
                precond_ref[:, columns] = jnp.dot(
                    residual_ref[:, of_mine], halves[2 * distance - 2][...], preferred_element_type=F32
                ) + jnp.dot(
                    residual_ref[:, of_other], halves[2 * distance - 1][...], preferred_element_type=F32
                )

        total_ref[...] += lax.dot_general(
            precond_ref[:, columns].astype(BF16), subspace_ref[:, columns], ACROSS,
            preferred_element_type=F32,
        )

    corr_ref[...] = total_ref[...].astype(corr_ref.dtype)


def first_kernel(width, precond_ref, coef_ref, subspace_ref, first_ref, corr_ref, total_ref):
    total_ref[...] = jnp.zeros_like(total_ref)

    @pl.loop(0, precond_ref.shape[1] // width)
    def _(b):
        columns = pl.ds(pl.multiple_of(b * width, width), width)
        basis = subspace_ref[:, columns]
        first = precond_ref[:, columns] - jnp.dot(coef_ref[...], basis, preferred_element_type=F32)
        first_ref[:, columns] = first
        total_ref[...] += lax.dot_general(first.astype(BF16), basis, ACROSS, preferred_element_type=F32)

    corr_ref[...] = total_ref[...].astype(corr_ref.dtype)


def last_kernel(width, first_ref, coef_ref, subspace_ref, out_ref):
    @pl.loop(0, first_ref.shape[1] // width)
    def _(b):
        columns = pl.ds(pl.multiple_of(b * width, width), width)
        out_ref[:, columns] = first_ref[:, columns] - jnp.dot(
            coef_ref[...], subspace_ref[:, columns], preferred_element_type=F32
        )


PARAMS = pltpu.CompilerParams(vmem_limit_bytes=24 * 1024 * 1024)


def per_device(residual, subspace, inverses, owner_offset, listed):
    roots, columns = residual.shape
    vectors = subspace.shape[0]
    inverse = inverses[0]
    size = inverse.shape[0]
    core = lax.axis_index("root")
    half = size // lax.axis_size("root")
    my_half = lax.dynamic_slice_in_dim(inverse, core * half, half, 0)
    fetched = [from_ahead(my_half, distance) for distance in range(1, OFFS)]
    halves = []
    for block in fetched:
        halves += [block, other_core(block)]

    corr_shape = jax.ShapeDtypeStruct((roots, vectors), BF16)
    wide = jax.ShapeDtypeStruct((roots, columns), F32)
    total = [pltpu.VMEM((roots, vectors), F32)]
    precond, corr = pl.pallas_call(
        precond_kernel,
        out_shape=(wide, corr_shape),
        in_specs=[SMEM] * 3 + [VMEM] * (3 + len(halves)),
        out_specs=(VMEM, VMEM),
        scratch_shapes=total,
        compiler_params=PARAMS,
    )(owner_offset, listed, core.astype(jnp.int32)[None], residual, subspace, inverse, *halves)
    coef = sum_over_tr(corr)

    def body(kernel):
        def call(*refs):
            kernel(size, *refs)
        return call

    first, corr = pl.pallas_call(
        body(first_kernel),
        out_shape=(wide, corr_shape),
        in_specs=[VMEM] * 3,
        out_specs=(VMEM, VMEM),
        scratch_shapes=total,
        compiler_params=PARAMS,
    )(precond, coef, subspace)
    coef = sum_over_tr(corr)
    return pl.pallas_call(
        body(last_kernel),
        out_shape=wide,
        in_specs=[VMEM] * 3,
        out_specs=VMEM,
        compiler_params=PARAMS,
    )(first, coef, subspace)


def solution(mesh):
    return jax.shard_map(
        per_device,
        mesh=mesh,
        in_specs=(
            P("root", ("grp", "tr")),
            P(None, ("grp", "tr")),
            P(("grp", "tr"), None, None),
            P(("grp", "tr")),
            P(("grp", "tr")),
        ),
        out_specs=P("root", ("grp", "tr")),
        check_vma=False,
    )
```

```python
import functools

import jax
import jax.numpy as jnp
from jax import lax
from jax.experimental import pallas as pl
from jax.experimental.pallas import tpu as pltpu
from jax.sharding import PartitionSpec as P

F32 = jnp.float32
BF16 = jnp.bfloat16
VMEM = pl.BlockSpec(memory_space=pltpu.VMEM)
SMEM = pl.BlockSpec(memory_space=pltpu.SMEM)
HBM = pl.BlockSpec(memory_space=pltpu.HBM)
ACROSS = (((1,), (1,)), ((), ()))
AHEAD, MIXED, SWAPPED = range(3)


def permute(block, source):
    n = lax.axis_size("tr")
    return lax.ppermute(block, "tr", [(source(i) % n, i) for i in range(n)])


def other_core(block):
    return lax.ppermute(block, "root", [(0, 1), (1, 0)])


def sum_over_tr(part):
    step = 1
    while step < lax.axis_size("tr"):
        part = part + permute(part, lambda i: i ^ step)
        step *= 2
    return part


def correlate(block, basis):
    return lax.dot_general(block.astype(BF16), basis, ACROSS, preferred_element_type=F32)


def chunk(b, size):
    return pl.ds(b * size, size)


def offset_of(kind):
    odd = lax.axis_index("tr") % 2
    return {AHEAD: 2, MIXED: 1 + 2 * odd, SWAPPED: 3 - 2 * odd}[kind]


def stage_kernel(
    offset_ref, listed_ref, residual_hbm, subspace_hbm, own_hbm,
    residual_ref, subspace_ref, precond_ref, corr_ref, own_ref, sems,
):
    size = own_ref.shape[0]
    count = residual_ref.shape[1] // size
    pltpu.make_async_copy(own_hbm, own_ref, sems.at[2 * count]).start()
    copies = []
    for b in range(count):
        columns = chunk(b, size)
        pair = [
            pltpu.make_async_copy(residual_hbm.at[:, columns], residual_ref.at[:, columns], sems.at[2 * b]),
            pltpu.make_async_copy(subspace_hbm.at[:, columns], subspace_ref.at[:, columns], sems.at[2 * b + 1]),
        ]
        for copy in pair:
            copy.start()
        copies.append(pair)
    corr_ref[...] = jnp.zeros_like(corr_ref)
    pltpu.make_async_copy(own_hbm, own_ref, sems.at[2 * count]).wait()
    for b in range(count):
        columns = chunk(b, size)
        for copy in copies[b]:
            copy.wait()

        listed = listed_ref[b] > 0
        own = jnp.logical_and(listed, offset_ref[b] == 0)

        @pl.when(own)
        def _():
            precond_ref[:, columns] = jnp.dot(
                residual_ref[:, columns], own_ref[...], preferred_element_type=F32
            )

        @pl.when(jnp.logical_not(listed))
        def _():
            precond_ref[:, columns] = residual_ref[:, columns].astype(F32)

        @pl.when(jnp.logical_or(own, jnp.logical_not(listed)))
        def _():
            corr_ref[...] += correlate(precond_ref[:, columns], subspace_ref[:, columns])


def fetched_kernel(kinds, offset_ref, listed_ref, residual_ref, subspace_ref, *rest):
    halves, (_, corr_in, precond_ref, corr_ref) = rest[: 2 * len(kinds)], rest[2 * len(kinds) :]
    half = halves[0].shape[0]
    size = 2 * half
    mine = lax.axis_index("root") * half
    corr_ref[...] = corr_in[...]
    for b in range(residual_ref.shape[1] // size):
        columns = chunk(b, size)
        of_mine = pl.ds(pl.multiple_of(b * size + mine, half), half)
        of_other = pl.ds(pl.multiple_of(b * size + half - mine, half), half)
        for k, kind in enumerate(kinds):
            @pl.when(jnp.logical_and(listed_ref[b] > 0, offset_ref[b] == offset_of(kind)))
            def _():
                solved = jnp.dot(
                    residual_ref[:, of_mine], halves[2 * k][...], preferred_element_type=F32
                ) + jnp.dot(
                    residual_ref[:, of_other], halves[2 * k + 1][...], preferred_element_type=F32
                )
                precond_ref[:, columns] = solved
                corr_ref[...] += correlate(solved, subspace_ref[:, columns])


def first_kernel(size, precond_ref, coef_ref, subspace_ref, first_ref, corr_ref):
    total = jnp.zeros(coef_ref.shape, F32)
    for b in range(precond_ref.shape[1] // size):
        columns = chunk(b, size)
        basis = subspace_ref[:, columns]
        first = precond_ref[:, columns] - jnp.dot(coef_ref[...], basis, preferred_element_type=F32)
        first_ref[:, columns] = first
        total += correlate(first, basis)
    corr_ref[...] = total.astype(corr_ref.dtype)


def last_kernel(size, first_ref, coef_ref, subspace_ref, out_hbm, out_ref, sems):
    copies = []
    for b in range(first_ref.shape[1] // size):
        columns = chunk(b, size)
        out_ref[:, columns] = first_ref[:, columns] - jnp.dot(
            coef_ref[...], subspace_ref[:, columns], preferred_element_type=F32
        )
        copy = pltpu.make_async_copy(out_ref.at[:, columns], out_hbm.at[:, columns], sems.at[b])
        copy.start()
        copies.append(copy)
    for copy in copies:
        copy.wait()


PARAMS = pltpu.CompilerParams(vmem_limit_bytes=24 * 1024 * 1024)


def cost(flops, bytes_accessed):
    return pl.CostEstimate(flops=flops, bytes_accessed=bytes_accessed, transcendentals=0)


def per_device(residual, subspace, inverses, owner_offset, listed):
    roots, columns = residual.shape
    vectors = subspace.shape[0]
    own = inverses[0]
    size = own.shape[0]
    count = columns // size
    core = lax.axis_index("root").astype(jnp.int32)
    half = size // lax.axis_size("root")

    wide = jax.ShapeDtypeStruct((roots, columns), F32)
    small = jax.ShapeDtypeStruct((roots, vectors), F32)
    sent = jax.ShapeDtypeStruct((roots, vectors), BF16)

    my_half = lax.dynamic_slice_in_dim(own, core * half, half, 0)
    mixed = permute(my_half, lambda i: i + 1 + 2 * (i % 2))
    ahead = permute(my_half, lambda i: i + 2)
    residual, subspace, precond, corr = pl.pallas_call(
        stage_kernel,
        out_shape=(
            jax.ShapeDtypeStruct(residual.shape, BF16),
            jax.ShapeDtypeStruct(subspace.shape, BF16),
            wide,
            small,
        ),
        in_specs=[SMEM, SMEM, HBM, HBM, HBM],
        out_specs=(VMEM,) * 4,
        scratch_shapes=[pltpu.VMEM((size, size), BF16), pltpu.SemaphoreType.DMA((2 * count + 1,))],
        cost_estimate=cost(4 * roots * vectors * columns, 16 * vectors * columns),
        compiler_params=pltpu.CompilerParams(vmem_limit_bytes=46 * 1024 * 1024),
    )(owner_offset, listed, residual, subspace, own)

    def fetched(kinds, halves, precond, corr):
        return pl.pallas_call(
            functools.partial(fetched_kernel, kinds),
            out_shape=(wide, small),
            in_specs=[SMEM] * 2 + [VMEM] * (4 + len(halves)),
            out_specs=(VMEM, VMEM),
            input_output_aliases={4 + len(halves): 0},
            cost_estimate=cost(0, 0),
            compiler_params=PARAMS,
        )(owner_offset, listed, residual, subspace, *halves, precond, corr)

    swapped = permute(ahead, lambda i: i ^ 1)
    mixed, corr = lax.optimization_barrier((mixed, corr))
    precond, corr = fetched(
        (AHEAD, MIXED, SWAPPED),
        (ahead, other_core(ahead), mixed, other_core(mixed), swapped, other_core(swapped)),
        precond, corr,
    )
    coef = sum_over_tr(corr.astype(BF16))

    def body(kernel):
        def call(*refs):
            kernel(size, *refs)
        return call

    first, corr = pl.pallas_call(
        body(first_kernel),
        out_shape=(wide, sent),
        in_specs=[VMEM] * 3,
        out_specs=(VMEM, VMEM),
        compiler_params=PARAMS,
    )(precond, coef, subspace)
    coef = sum_over_tr(corr)
    return pl.pallas_call(
        body(last_kernel),
        out_shape=wide,
        in_specs=[VMEM] * 3,
        out_specs=HBM,
        scratch_shapes=[pltpu.VMEM((roots, columns), F32), pltpu.SemaphoreType.DMA((count,))],
        compiler_params=PARAMS,
    )(first, coef, subspace)


def solution(mesh):
    return jax.shard_map(
        per_device,
        mesh=mesh,
        in_specs=(
            P("root", ("grp", "tr")),
            P(None, ("grp", "tr")),
            P(("grp", "tr"), None, None),
            P(("grp", "tr")),
            P(("grp", "tr")),
        ),
        out_specs=P("root", ("grp", "tr")),
        check_vma=False,
    )
```

```python
import functools

import jax
import jax.numpy as jnp
from jax import lax
from jax.experimental import pallas as pl
from jax.experimental.pallas import tpu as pltpu
from jax.sharding import PartitionSpec as P

F32 = jnp.float32
BF16 = jnp.bfloat16
VMEM = pl.BlockSpec(memory_space=pltpu.VMEM)
SMEM = pl.BlockSpec(memory_space=pltpu.SMEM)
HBM = pl.BlockSpec(memory_space=pltpu.HBM)
ACROSS = (((1,), (1,)), ((), ()))
AHEAD, MIXED, SWAPPED = range(3)


def permute(block, source):
    n = lax.axis_size("tr")
    return lax.ppermute(block, "tr", [(source(i) % n, i) for i in range(n)])


def permute_cores(block, source):
    n, cores = lax.axis_size("tr"), lax.axis_size("root")
    pairs = []
    for i in range(n):
        for core in range(cores):
            at, of = source(i, core)
            pairs.append((at % n * cores + of, i * cores + core))
    return lax.ppermute(block, ("tr", "root"), pairs)


def other_core(block):
    return lax.ppermute(block, "root", [(0, 1), (1, 0)])


PAD = 16


def diagonal(rows, half):
    row = lax.broadcasted_iota(jnp.int32, rows, 0) + half * rows[0]
    return row == lax.broadcasted_iota(jnp.int32, rows, 1)


def encode(message_ref, values, half):
    count = values.shape[0]
    rounded = values.astype(BF16)
    lost = jnp.where(diagonal(values.shape, half), values - rounded.astype(F32), 0.0)
    lost = jnp.sum(lost, axis=0, keepdims=True)
    message_ref[:count, :] = rounded
    message_ref[count:, :] = jnp.broadcast_to(lost, (PAD, values.shape[1])).astype(BF16)


def decode(message_ref, half):
    count = message_ref.shape[0] - PAD
    values = message_ref[:count, :].astype(F32)
    lost = message_ref[count : count + 1, :].astype(F32)
    return values + jnp.where(diagonal(values.shape, half), lost, 0.0)


def gram_kernel(subspace_hbm, subspace_ref, kept_ref, message_ref, gram_ref, sems):
    vectors, columns = subspace_hbm.shape
    core = lax.axis_index("root")
    block = vectors // 2
    part = block // 2
    pieces = sems.shape[0]
    width = columns // pieces
    copies = [
        pltpu.make_async_copy(
            subspace_hbm.at[:, chunk(b, width)], subspace_ref.at[:, chunk(b, width)], sems.at[b]
        )
        for b in range(pieces)
    ]
    for copy in copies:
        copy.start()
    for b in range(pieces):
        copies[b].wait()
        span = chunk(b, width)
        of_core = subspace_ref[pl.ds(pl.multiple_of(core * block, block), block), span]
        of_part = subspace_ref[pl.ds(pl.multiple_of(core * part, part), part), span]
        top, bottom = correlate(of_core, of_core), correlate(of_part, subspace_ref[block:, span])
        if b == 0:
            gram_ref[:block, :] = top
            gram_ref[block:, :] = bottom
        else:
            gram_ref[:block, :] += top
            gram_ref[block:, :] += bottom
    half = lax.axis_index("tr") % 2
    count = kept_ref.shape[0]
    kept_ref[...] = gram_ref[pl.ds(pl.multiple_of(half * count, count), count), :]
    given = gram_ref[pl.ds(pl.multiple_of((1 - half) * count, count), count), :]
    encode(message_ref, given, 1 - half)


def kept_kernel(kept_ref, got_ref, message_ref):
    half = lax.axis_index("tr") % 2
    encode(message_ref, kept_ref[...] + decode(got_ref, half), half)


def add_kernel(sent_ref, got_ref, message_ref):
    half = lax.axis_index("tr") % 2
    encode(message_ref, decode(sent_ref, half) + decode(got_ref, half), half)


def assemble_kernel(mine_ref, got_ref, mine_other_ref, got_other_ref, gram_ref, lost_ref, packed_ref):
    half = lax.axis_index("tr") % 2
    core = lax.axis_index("root")
    count = mine_ref.shape[0] - PAD
    block = mine_ref.shape[1]
    part = block // 2
    for owner, near_ref, far_ref in ((core, mine_ref, got_ref), (1 - core, mine_other_ref, got_other_ref)):
        packed_ref[pl.ds(pl.multiple_of(half * count, count), count), :] = near_ref[:count, :]
        packed_ref[pl.ds(pl.multiple_of((1 - half) * count, count), count), :] = far_ref[:count, :]
        at = pl.ds(pl.multiple_of(owner * block, block), block)
        gram_ref[at, at] = packed_ref[:block, :]
        gram_ref[pl.ds(pl.multiple_of(owner * part, part), part), block:] = packed_ref[block:, :]
        lost = near_ref[count : count + 8, :].astype(F32) + far_ref[count : count + 8, :].astype(F32)
        lost_ref[:, at] = lost


def correlate(block, basis):
    return lax.dot_general(block.astype(BF16), basis, ACROSS, preferred_element_type=F32)


def chunk(b, size):
    return pl.ds(b * size, size)


def offset_of(kind):
    odd = lax.axis_index("tr") % 2
    return {AHEAD: 2, MIXED: 1 + 2 * odd, SWAPPED: 3 - 2 * odd}[kind]


def local_kernel(offset_ref, listed_ref, residual_ref, subspace_ref, own_ref, precond_ref, corr_ref):
    size = own_ref.shape[0]
    corr_ref[...] = jnp.zeros_like(corr_ref)
    for b in range(residual_ref.shape[1] // size):
        columns = chunk(b, size)
        listed = listed_ref[b] > 0
        own = jnp.logical_and(listed, offset_ref[b] == 0)

        @pl.when(own)
        def _():
            precond_ref[:, columns] = jnp.dot(
                residual_ref[:, columns], own_ref[...], preferred_element_type=F32
            )

        @pl.when(jnp.logical_not(listed))
        def _():
            precond_ref[:, columns] = residual_ref[:, columns].astype(F32)

        @pl.when(jnp.logical_or(own, jnp.logical_not(listed)))
        def _():
            corr_ref[...] += correlate(precond_ref[:, columns], subspace_ref[:, columns])


def fetched_kernel(kinds, offset_ref, listed_ref, residual_ref, subspace_ref, *rest):
    halves, (_, corr_in, precond_ref, corr_ref) = rest[: 2 * len(kinds)], rest[2 * len(kinds) :]
    half = halves[0].shape[0]
    size = 2 * half
    mine = lax.axis_index("root") * half
    corr_ref[...] = corr_in[...]
    for b in range(residual_ref.shape[1] // size):
        columns = chunk(b, size)
        of_mine = pl.ds(pl.multiple_of(b * size + mine, half), half)
        of_other = pl.ds(pl.multiple_of(b * size + half - mine, half), half)
        for k, kind in enumerate(kinds):
            @pl.when(jnp.logical_and(listed_ref[b] > 0, offset_ref[b] == offset_of(kind)))
            def _():
                solved = jnp.dot(
                    residual_ref[:, of_mine], halves[2 * k][...], preferred_element_type=F32
                ) + jnp.dot(
                    residual_ref[:, of_other], halves[2 * k + 1][...], preferred_element_type=F32
                )
                precond_ref[:, columns] = solved
                corr_ref[...] += correlate(solved, subspace_ref[:, columns])


def last_kernel(size, precond_ref, corr_ref, got_ref, gram_ref, lost_ref, subspace_ref, out_hbm, out_ref, sems):
    corr = corr_ref[...].astype(F32) + got_ref[...].astype(F32)
    block = gram_ref.shape[0] // 2
    coef = corr.astype(BF16)
    left, right = coef[:, :block], coef[:, block:]
    off = gram_ref[:block, block:]
    again = jnp.concatenate(
        [
            jnp.dot(left, gram_ref[:block, :block], preferred_element_type=F32)
            + lax.dot_general(right, off, ACROSS, preferred_element_type=F32),
            jnp.dot(left, off, preferred_element_type=F32)
            + jnp.dot(right, gram_ref[block:, block:], preferred_element_type=F32),
        ],
        axis=1,
    )
    coef_2 = corr - again - coef.astype(F32) * lost_ref[0:1, :]
    total = coef.astype(F32) + coef_2
    lead = total.astype(BF16)
    trail = (total - lead.astype(F32)).astype(BF16)
    copies = []
    for b in range(precond_ref.shape[1] // size):
        columns = chunk(b, size)
        basis = subspace_ref[:, columns]
        out_ref[:, columns] = precond_ref[:, columns] - (
            jnp.dot(lead, basis, preferred_element_type=F32)
            + jnp.dot(trail, basis, preferred_element_type=F32)
        )
        copy = pltpu.make_async_copy(out_ref.at[:, columns], out_hbm.at[:, columns], sems.at[b])
        copy.start()
        copies.append(copy)
    for copy in copies:
        copy.wait()


PARAMS = pltpu.CompilerParams(vmem_limit_bytes=24 * 1024 * 1024)


def cost(flops, bytes_accessed):
    return pl.CostEstimate(flops=flops, bytes_accessed=bytes_accessed, transcendentals=0)


def per_device(residual, subspace, inverses, owner_offset, listed):
    roots, columns = residual.shape
    vectors = subspace.shape[0]
    own = inverses[0]
    size = own.shape[0]
    count = columns // size
    core = lax.axis_index("root").astype(jnp.int32)
    half = size // lax.axis_size("root")

    block = vectors // 2
    count_half = (block + block // 2) // 2

    def shape(*dims, dtype=BF16):
        return jax.ShapeDtypeStruct(dims, dtype)

    wide = shape(roots, columns, dtype=F32)
    small = shape(roots, vectors, dtype=F32)
    message = shape(count_half + PAD, block)

    def call(kernel, outs, *args, scratch=(), **more):
        return pl.pallas_call(
            kernel,
            out_shape=outs,
            in_specs=[VMEM] * len(args),
            out_specs=jax.tree.map(lambda _: VMEM, outs),
            scratch_shapes=list(scratch),
            compiler_params=PARAMS,
            **more,
        )(*args)

    my_half = lax.dynamic_slice_in_dim(own, core * half, half, 0)
    ahead = permute(my_half, lambda i: i + 2)
    mixed = permute_cores(my_half, lambda i, core: (i ^ 1, 1) if core else (i + 1 + 2 * (i % 2), 0))

    subspace, kept, given = pl.pallas_call(
        gram_kernel,
        out_shape=(shape(*subspace.shape), shape(count_half, block, dtype=F32), message),
        in_specs=[HBM],
        out_specs=(VMEM,) * 3,
        scratch_shapes=[pltpu.VMEM((2 * count_half, block), F32), pltpu.SemaphoreType.DMA((4,))],
        cost_estimate=cost(2 * vectors * vectors * columns, 16 * vectors * columns),
        compiler_params=pltpu.CompilerParams(vmem_limit_bytes=46 * 1024 * 1024),
    )(subspace)
    gram = call(kept_kernel, message, kept, permute(given, lambda i: i ^ 1))
    ahead, gram = lax.optimization_barrier((ahead, gram))
    swapped = permute(ahead, lambda i: i ^ 1)
    gram = call(add_kernel, message, gram, permute(gram, lambda i: i ^ 2))
    mixed = permute_cores(mixed, lambda i, core: (i + 4, 1) if core and i % 2 else (i, core))
    mixed, swapped, gram = lax.optimization_barrier((mixed, swapped, gram))
    step = 4
    while step < lax.axis_size("tr"):
        gram = call(add_kernel, message, gram, permute(gram, lambda i: i ^ step))
        step *= 2

    precond, corr = pl.pallas_call(
        local_kernel,
        out_shape=(wide, small),
        in_specs=[SMEM, SMEM, VMEM, VMEM, VMEM],
        out_specs=(VMEM,) * 2,
        compiler_params=PARAMS,
    )(owner_offset, listed, residual, subspace, own)

    def fetched(kinds, halves, precond, corr):
        return pl.pallas_call(
            functools.partial(fetched_kernel, kinds),
            out_shape=(wide, small),
            in_specs=[SMEM] * 2 + [VMEM] * (4 + len(halves)),
            out_specs=(VMEM, VMEM),
            input_output_aliases={4 + len(halves): 0},
            cost_estimate=cost(0, 0),
            compiler_params=PARAMS,
        )(owner_offset, listed, residual, subspace, *halves, precond, corr)

    mixed, corr = lax.optimization_barrier((mixed, corr))
    precond, corr = fetched(
        (AHEAD, MIXED, SWAPPED),
        (ahead, other_core(ahead), mixed, other_core(mixed), swapped, other_core(swapped)),
        precond, corr,
    )
    gram_far = permute(gram, lambda i: i ^ 1)
    gram, lost = call(
        assemble_kernel,
        (shape(vectors, vectors), shape(8, vectors, dtype=F32)),
        gram, gram_far, other_core(gram), other_core(gram_far),
        scratch=[pltpu.VMEM((2 * count_half, block), BF16)],
    )

    corr = corr.astype(BF16)
    step = 1
    while 2 * step < lax.axis_size("tr"):
        corr = corr + permute(corr, lambda i: i ^ step)
        step *= 2
    got = permute(corr, lambda i: i ^ step)

    def last(*refs):
        last_kernel(size, *refs)

    return pl.pallas_call(
        last,
        out_shape=wide,
        in_specs=[VMEM] * 6,
        out_specs=HBM,
        scratch_shapes=[pltpu.VMEM((roots, columns), F32), pltpu.SemaphoreType.DMA((count,))],
        compiler_params=PARAMS,
    )(precond, corr, got, gram, lost, subspace)


def solution(mesh):
    return jax.shard_map(
        per_device,
        mesh=mesh,
        in_specs=(
            P("root", ("grp", "tr")),
            P(None, ("grp", "tr")),
            P(("grp", "tr"), None, None),
            P(("grp", "tr")),
            P(("grp", "tr")),
        ),
        out_specs=P("root", ("grp", "tr")),
        check_vma=False,
    )
```

```python
import functools

import jax
import jax.numpy as jnp
from jax import lax
from jax.experimental import pallas as pl
from jax.experimental.pallas import tpu as pltpu
from jax.sharding import PartitionSpec as P

F32 = jnp.float32
BF16 = jnp.bfloat16
VMEM = pl.BlockSpec(memory_space=pltpu.VMEM)
SMEM = pl.BlockSpec(memory_space=pltpu.SMEM)
HBM = pl.BlockSpec(memory_space=pltpu.HBM)
ACROSS = (((1,), (1,)), ((), ()))
AHEAD, MIXED, SWAPPED = range(3)


def permute(block, source):
    n = lax.axis_size("tr")
    return lax.ppermute(block, "tr", [(source(i) % n, i) for i in range(n)])


def permute_cores(block, source):
    n, cores = lax.axis_size("tr"), lax.axis_size("root")
    pairs = []
    for i in range(n):
        for core in range(cores):
            at, of = source(i, core)
            pairs.append((at % n * cores + of, i * cores + core))
    return lax.ppermute(block, ("tr", "root"), pairs)


def other_core(block):
    return lax.ppermute(block, "root", [(0, 1), (1, 0)])


PAD = 16


def diagonal(rows, half):
    row = lax.broadcasted_iota(jnp.int32, rows, 0) + half * rows[0]
    return row == lax.broadcasted_iota(jnp.int32, rows, 1)


def encode(message_ref, values, half):
    count = values.shape[0]
    rounded = values.astype(BF16)
    lost = jnp.where(diagonal(values.shape, half), values - rounded.astype(F32), 0.0)
    lost = jnp.sum(lost, axis=0, keepdims=True)
    message_ref[:count, :] = rounded
    message_ref[count:, :] = jnp.broadcast_to(lost, (PAD, values.shape[1])).astype(BF16)


def decode(message_ref, half):
    count = message_ref.shape[0] - PAD
    values = message_ref[:count, :].astype(F32)
    lost = message_ref[count : count + 1, :].astype(F32)
    return values + jnp.where(diagonal(values.shape, half), lost, 0.0)


def gram_kernel(subspace_hbm, subspace_ref, kept_ref, message_ref, gram_ref, sems):
    vectors, columns = subspace_hbm.shape
    core = lax.axis_index("root")
    block = vectors // 2
    part = block // 2
    pieces = sems.shape[0]
    width = columns // pieces
    copies = [
        pltpu.make_async_copy(
            subspace_hbm.at[:, chunk(b, width)], subspace_ref.at[:, chunk(b, width)], sems.at[b]
        )
        for b in range(pieces)
    ]
    for copy in copies:
        copy.start()
    for b in range(pieces):
        copies[b].wait()
        span = chunk(b, width)
        of_core = subspace_ref[pl.ds(pl.multiple_of(core * block, block), block), span]
        of_part = subspace_ref[pl.ds(pl.multiple_of(core * part, part), part), span]
        top, bottom = correlate(of_core, of_core), correlate(of_part, subspace_ref[block:, span])
        if b == 0:
            gram_ref[:block, :] = top
            gram_ref[block:, :] = bottom
        else:
            gram_ref[:block, :] += top
            gram_ref[block:, :] += bottom
    half = lax.axis_index("tr") % 2
    count = kept_ref.shape[0]
    kept_ref[...] = gram_ref[pl.ds(pl.multiple_of(half * count, count), count), :]
    given = gram_ref[pl.ds(pl.multiple_of((1 - half) * count, count), count), :]
    encode(message_ref, given, 1 - half)


def kept_kernel(kept_ref, got_ref, message_ref):
    half = lax.axis_index("tr") % 2
    encode(message_ref, kept_ref[...] + decode(got_ref, half), half)


def add_kernel(sent_ref, got_ref, message_ref):
    half = lax.axis_index("tr") % 2
    encode(message_ref, decode(sent_ref, half) + decode(got_ref, half), half)


def assemble_kernel(mine_ref, got_ref, mine_other_ref, got_other_ref, gram_ref, lost_ref, packed_ref):
    half = lax.axis_index("tr") % 2
    core = lax.axis_index("root")
    count = mine_ref.shape[0] - PAD
    block = mine_ref.shape[1]
    part = block // 2
    for owner, near_ref, far_ref in ((core, mine_ref, got_ref), (1 - core, mine_other_ref, got_other_ref)):
        packed_ref[pl.ds(pl.multiple_of(half * count, count), count), :] = near_ref[:count, :]
        packed_ref[pl.ds(pl.multiple_of((1 - half) * count, count), count), :] = far_ref[:count, :]
        at = pl.ds(pl.multiple_of(owner * block, block), block)
        gram_ref[at, at] = packed_ref[:block, :]
        gram_ref[pl.ds(pl.multiple_of(owner * part, part), part), block:] = packed_ref[block:, :]
        lost = near_ref[count : count + 8, :].astype(F32) + far_ref[count : count + 8, :].astype(F32)
        lost_ref[:, at] = lost


def correlate(block, basis):
    return lax.dot_general(block.astype(BF16), basis, ACROSS, preferred_element_type=F32)


def chunk(b, size):
    return pl.ds(b * size, size)


def offset_of(kind):
    odd = lax.axis_index("tr") % 2
    return {AHEAD: 2, MIXED: 1 + 2 * odd, SWAPPED: 3 - 2 * odd}[kind]


def local_kernel(offset_ref, listed_ref, residual_ref, subspace_ref, own_ref, precond_ref, corr_ref):
    size = own_ref.shape[0]
    corr_ref[...] = jnp.zeros_like(corr_ref)
    for b in range(residual_ref.shape[1] // size):
        columns = chunk(b, size)
        listed = listed_ref[b] > 0
        own = jnp.logical_and(listed, offset_ref[b] == 0)

        @pl.when(own)
        def _():
            precond_ref[:, columns] = jnp.dot(
                residual_ref[:, columns], own_ref[...], preferred_element_type=F32
            )

        @pl.when(jnp.logical_not(listed))
        def _():
            precond_ref[:, columns] = residual_ref[:, columns].astype(F32)

        @pl.when(jnp.logical_or(own, jnp.logical_not(listed)))
        def _():
            corr_ref[...] += correlate(precond_ref[:, columns], subspace_ref[:, columns])


def fetched_kernel(kinds, offset_ref, listed_ref, residual_ref, subspace_ref, *rest):
    halves, (_, corr_in, precond_ref, corr_ref) = rest[: 2 * len(kinds)], rest[2 * len(kinds) :]
    half = halves[0].shape[0]
    size = 2 * half
    mine = lax.axis_index("root") * half
    corr_ref[...] = corr_in[...]
    for b in range(residual_ref.shape[1] // size):
        columns = chunk(b, size)
        of_mine = pl.ds(pl.multiple_of(b * size + mine, half), half)
        of_other = pl.ds(pl.multiple_of(b * size + half - mine, half), half)
        for k, kind in enumerate(kinds):
            @pl.when(jnp.logical_and(listed_ref[b] > 0, offset_ref[b] == offset_of(kind)))
            def _():
                solved = jnp.dot(
                    residual_ref[:, of_mine], halves[2 * k][...], preferred_element_type=F32
                ) + jnp.dot(
                    residual_ref[:, of_other], halves[2 * k + 1][...], preferred_element_type=F32
                )
                precond_ref[:, columns] = solved
                corr_ref[...] += correlate(solved, subspace_ref[:, columns])


def last_kernel(size, precond_ref, corr_ref, got_ref, gram_ref, lost_ref, subspace_ref, out_hbm, out_ref, sems):
    corr = corr_ref[...].astype(F32) + got_ref[...].astype(F32)
    block = gram_ref.shape[0] // 2
    coef = corr.astype(BF16)
    left, right = coef[:, :block], coef[:, block:]
    off = gram_ref[:block, block:]
    again = jnp.concatenate(
        [
            jnp.dot(left, gram_ref[:block, :block], preferred_element_type=F32)
            + lax.dot_general(right, off, ACROSS, preferred_element_type=F32),
            jnp.dot(left, off, preferred_element_type=F32)
            + jnp.dot(right, gram_ref[block:, block:], preferred_element_type=F32),
        ],
        axis=1,
    )
    coef_2 = corr - again - coef.astype(F32) * lost_ref[0:1, :]
    total = coef.astype(F32) + coef_2
    lead = total.astype(BF16)
    both = jnp.concatenate([lead, (total - lead.astype(F32)).astype(BF16)], axis=0)
    roots = lead.shape[0]
    copies = []
    for b in range(precond_ref.shape[1] // size):
        columns = chunk(b, size)
        basis = subspace_ref[:, columns]
        step = jnp.dot(both, basis, preferred_element_type=F32)
        out_ref[:, columns] = precond_ref[:, columns] - (step[:roots, :] + step[roots:, :])
        copy = pltpu.make_async_copy(out_ref.at[:, columns], out_hbm.at[:, columns], sems.at[b])
        copy.start()
        copies.append(copy)
    for copy in copies:
        copy.wait()


PARAMS = pltpu.CompilerParams(vmem_limit_bytes=24 * 1024 * 1024)


def cost(flops, bytes_accessed):
    return pl.CostEstimate(flops=flops, bytes_accessed=bytes_accessed, transcendentals=0)


def per_device(residual, subspace, inverses, owner_offset, listed):
    roots, columns = residual.shape
    vectors = subspace.shape[0]
    own = inverses[0]
    size = own.shape[0]
    count = columns // size
    core = lax.axis_index("root").astype(jnp.int32)
    half = size // lax.axis_size("root")

    block = vectors // 2
    count_half = (block + block // 2) // 2

    def shape(*dims, dtype=BF16):
        return jax.ShapeDtypeStruct(dims, dtype)

    wide = shape(roots, columns, dtype=F32)
    small = shape(roots, vectors, dtype=F32)
    message = shape(count_half + PAD, block)

    def call(kernel, outs, *args, scratch=(), **more):
        return pl.pallas_call(
            kernel,
            out_shape=outs,
            in_specs=[VMEM] * len(args),
            out_specs=jax.tree.map(lambda _: VMEM, outs),
            scratch_shapes=list(scratch),
            compiler_params=PARAMS,
            **more,
        )(*args)

    my_half = lax.dynamic_slice_in_dim(own, core * half, half, 0)
    ahead = permute(my_half, lambda i: i + 2)
    mixed = permute_cores(my_half, lambda i, core: (i ^ core, core))

    subspace, kept, given = pl.pallas_call(
        gram_kernel,
        out_shape=(shape(*subspace.shape), shape(count_half, block, dtype=F32), message),
        in_specs=[HBM],
        out_specs=(VMEM,) * 3,
        scratch_shapes=[pltpu.VMEM((2 * count_half, block), F32), pltpu.SemaphoreType.DMA((4,))],
        cost_estimate=cost(2 * vectors * vectors * columns, 16 * vectors * columns),
        compiler_params=pltpu.CompilerParams(vmem_limit_bytes=46 * 1024 * 1024),
    )(subspace)
    mixed, kept = lax.optimization_barrier((mixed, kept))
    mixed = permute_cores(
        mixed,
        lambda i, core: ((i + 4, 1) if i % 2 else (i, 1)) if core else (i + 1 + 2 * (i % 2), 0),
    )
    gram = call(kept_kernel, message, kept, permute(given, lambda i: i ^ 1))
    ahead, gram = lax.optimization_barrier((ahead, gram))
    swapped = permute(ahead, lambda i: i ^ 1)
    gram = call(add_kernel, message, gram, permute(gram, lambda i: i ^ 2))
    mixed, gram = lax.optimization_barrier((mixed, gram))
    step = 4
    while step < lax.axis_size("tr"):
        gram = call(add_kernel, message, gram, permute(gram, lambda i: i ^ step))
        step *= 2

    precond, corr = pl.pallas_call(
        local_kernel,
        out_shape=(wide, small),
        in_specs=[SMEM, SMEM, VMEM, VMEM, VMEM],
        out_specs=(VMEM,) * 2,
        compiler_params=PARAMS,
    )(owner_offset, listed, residual, subspace, own)

    def fetched(kinds, halves, precond, corr):
        return pl.pallas_call(
            functools.partial(fetched_kernel, kinds),
            out_shape=(wide, small),
            in_specs=[SMEM] * 2 + [VMEM] * (4 + len(halves)),
            out_specs=(VMEM, VMEM),
            input_output_aliases={4 + len(halves): 0},
            cost_estimate=cost(0, 0),
            compiler_params=PARAMS,
        )(owner_offset, listed, residual, subspace, *halves, precond, corr)

    mixed, corr = lax.optimization_barrier((mixed, corr))
    precond, corr = fetched(
        (AHEAD, MIXED, SWAPPED),
        (ahead, other_core(ahead), mixed, other_core(mixed), swapped, other_core(swapped)),
        precond, corr,
    )
    gram_far = permute(gram, lambda i: i ^ 1)
    gram, lost = call(
        assemble_kernel,
        (shape(vectors, vectors), shape(8, vectors, dtype=F32)),
        gram, gram_far, other_core(gram), other_core(gram_far),
        scratch=[pltpu.VMEM((2 * count_half, block), BF16)],
    )

    corr = corr.astype(BF16)
    step = 1
    while 2 * step < lax.axis_size("tr"):
        corr = corr + permute(corr, lambda i: i ^ step)
        step *= 2
    got = permute(corr, lambda i: i ^ step)

    def last(*refs):
        last_kernel(size, *refs)

    return pl.pallas_call(
        last,
        out_shape=wide,
        in_specs=[VMEM] * 6,
        out_specs=HBM,
        scratch_shapes=[pltpu.VMEM((roots, columns), F32), pltpu.SemaphoreType.DMA((count,))],
        compiler_params=PARAMS,
    )(precond, corr, got, gram, lost, subspace)


def solution(mesh):
    return jax.shard_map(
        per_device,
        mesh=mesh,
        in_specs=(
            P("root", ("grp", "tr")),
            P(None, ("grp", "tr")),
            P(("grp", "tr"), None, None),
            P(("grp", "tr")),
            P(("grp", "tr")),
        ),
        out_specs=P("root", ("grp", "tr")),
        check_vma=False,
    )
```

```python
import functools

import jax
import jax.numpy as jnp
from jax import lax
from jax.experimental import pallas as pl
from jax.experimental.pallas import tpu as pltpu
from jax.sharding import PartitionSpec as P

F32 = jnp.float32
BF16 = jnp.bfloat16
VMEM = pl.BlockSpec(memory_space=pltpu.VMEM)
SMEM = pl.BlockSpec(memory_space=pltpu.SMEM)
HBM = pl.BlockSpec(memory_space=pltpu.HBM)
ACROSS = (((1,), (1,)), ((), ()))
AHEAD, MIXED, SWAPPED = range(3)


def permute(block, source):
    n = lax.axis_size("tr")
    return lax.ppermute(block, "tr", [(source(i) % n, i) for i in range(n)])


def permute_cores(block, source):
    n, cores = lax.axis_size("tr"), lax.axis_size("root")
    pairs = []
    for i in range(n):
        for core in range(cores):
            at, of = source(i, core)
            pairs.append((at % n * cores + of, i * cores + core))
    return lax.ppermute(block, ("tr", "root"), pairs)


def other_core(block):
    return lax.ppermute(block, "root", [(0, 1), (1, 0)])


PAD = 16


def diagonal(rows, half):
    quarter = rows[1] // 2
    row = lax.broadcasted_iota(jnp.int32, rows, 0) + half * rows[0]
    column = lax.broadcasted_iota(jnp.int32, rows, 1)
    folded = row - 2 * quarter
    at_end = jnp.logical_and(
        folded >= 0, jnp.logical_or(column == folded, column == folded + quarter + quarter // 2)
    )
    return jnp.logical_or(at_end, jnp.logical_and(row < quarter, column == row))


def encode(message_ref, values, half):
    count = values.shape[0]
    rounded = values.astype(BF16)
    lost = jnp.where(diagonal(values.shape, half), values - rounded.astype(F32), 0.0)
    lost = jnp.sum(lost, axis=0, keepdims=True)
    message_ref[:count, :] = rounded
    message_ref[count:, :] = jnp.broadcast_to(lost, (PAD, values.shape[1])).astype(BF16)


def decode(message_ref, half):
    count = message_ref.shape[0] - PAD
    values = message_ref[:count, :].astype(F32)
    lost = message_ref[count:, :].astype(F32)[0:1, :]
    return values + jnp.where(diagonal(values.shape, half), lost, 0.0)


def gram_kernel(subspace_hbm, subspace_ref, kept_ref, message_ref, gram_ref, sems):
    vectors, columns = subspace_hbm.shape
    core = lax.axis_index("root")
    quarter = vectors // 4
    pieces = sems.shape[0]
    width = columns // pieces
    copies = [
        pltpu.make_async_copy(
            subspace_hbm.at[:, chunk(b, width)], subspace_ref.at[:, chunk(b, width)], sems.at[b]
        )
        for b in range(pieces)
    ]
    for copy in copies:
        copy.start()
    fold = quarter // 2
    for b in range(pieces):
        copies[b].wait()
        span = chunk(b, width)

        def rows(start, count):
            return subspace_ref[pl.ds(pl.multiple_of(start, quarter), count), span]

        near = correlate(rows(2 * core * quarter, 2 * quarter), rows(2 * core * quarter, 2 * quarter))
        far = correlate(rows(core * quarter, quarter), subspace_ref[2 * quarter :, span])
        parts = (
            (0, quarter, slice(None), near[:quarter, :]),
            (quarter, quarter, slice(None), far),
            (2 * quarter, fold, slice(0, quarter), near[quarter : quarter + fold, quarter:]),
            (2 * quarter, fold, slice(quarter, None), near[quarter + fold :, quarter:]),
        )
        for start, count, across, value in parts:
            if b == 0:
                gram_ref[start : start + count, across] = value
            else:
                gram_ref[start : start + count, across] += value
    half = lax.axis_index("tr") % 2
    count = kept_ref.shape[0]
    kept_ref[...] = gram_ref[pl.ds(pl.multiple_of(half * count, count), count), :]
    given = gram_ref[pl.ds(pl.multiple_of((1 - half) * count, count), count), :]
    encode(message_ref, given, 1 - half)


def kept_kernel(kept_ref, got_ref, message_ref):
    half = lax.axis_index("tr") % 2
    encode(message_ref, kept_ref[...] + decode(got_ref, half), half)


def add_kernel(sent_ref, got_ref, message_ref):
    half = lax.axis_index("tr") % 2
    encode(message_ref, decode(sent_ref, half) + decode(got_ref, half), half)


def assemble_kernel(mine_ref, got_ref, mine_other_ref, got_other_ref, gram_ref, lost_ref, packed_ref):
    half = lax.axis_index("tr") % 2
    core = lax.axis_index("root")
    count = mine_ref.shape[0] - PAD
    quarter = mine_ref.shape[1] // 2
    fold = quarter // 2
    for owner, near_ref, far_ref in ((core, mine_ref, got_ref), (1 - core, mine_other_ref, got_other_ref)):
        packed_ref[pl.ds(pl.multiple_of(half * count, count), count), :] = near_ref[:count, :].astype(F32)
        packed_ref[pl.ds(pl.multiple_of((1 - half) * count, count), count), :] = far_ref[:count, :].astype(F32)
        first = pl.ds(pl.multiple_of(2 * owner * quarter, quarter), quarter)
        second = pl.ds(pl.multiple_of(2 * owner * quarter + quarter, quarter), quarter)
        across = packed_ref[:quarter, quarter:]
        gram_ref[first, first] = packed_ref[:quarter, :quarter].astype(BF16)
        gram_ref[first, second] = across.astype(BF16)
        gram_ref[second, first] = across.T.astype(BF16)
        gram_ref[second, second] = jnp.concatenate(
            [packed_ref[2 * quarter :, :quarter], packed_ref[2 * quarter :, quarter:]], axis=0
        ).astype(BF16)
        to = pl.ds(pl.multiple_of(owner * quarter, quarter), quarter)
        outer = packed_ref[quarter : 2 * quarter, :]
        gram_ref[to, 2 * quarter :] = outer.astype(BF16)
        gram_ref[2 * quarter :, to] = outer.T.astype(BF16)
        lost_ref[:, first] = jnp.where(half == 0, near_ref[count:, :quarter], far_ref[count:, :quarter]).astype(F32)
        last = jnp.where(half == 0, far_ref[count:, :], near_ref[count:, :]).astype(F32)
        lane = lax.broadcasted_iota(jnp.int32, (PAD, quarter), 1)
        lost_ref[:, second] = jnp.where(lane < fold, last[:, :quarter], last[:, quarter:])


def correlate(block, basis):
    return lax.dot_general(block.astype(BF16), basis, ACROSS, preferred_element_type=F32)


def chunk(b, size):
    return pl.ds(b * size, size)


def offset_of(kind):
    odd = lax.axis_index("tr") % 2
    return {AHEAD: 2, MIXED: 1 + 2 * odd, SWAPPED: 3 - 2 * odd}[kind]


def local_kernel(offset_ref, listed_ref, residual_ref, subspace_ref, own_ref, precond_ref, corr_ref):
    size = own_ref.shape[0]
    corr_ref[...] = jnp.zeros_like(corr_ref)
    for b in range(residual_ref.shape[1] // size):
        columns = chunk(b, size)
        listed = listed_ref[b] > 0
        own = jnp.logical_and(listed, offset_ref[b] == 0)

        @pl.when(own)
        def _():
            precond_ref[:, columns] = jnp.dot(
                residual_ref[:, columns], own_ref[...], preferred_element_type=F32
            )

        @pl.when(jnp.logical_not(listed))
        def _():
            precond_ref[:, columns] = residual_ref[:, columns].astype(F32)

        @pl.when(jnp.logical_or(own, jnp.logical_not(listed)))
        def _():
            corr_ref[...] += correlate(precond_ref[:, columns], subspace_ref[:, columns])


def fetched_kernel(kinds, offset_ref, listed_ref, residual_ref, subspace_ref, *rest):
    halves, (_, corr_in, precond_ref, corr_ref) = rest[: 2 * len(kinds)], rest[2 * len(kinds) :]
    half = halves[0].shape[0]
    size = 2 * half
    mine = lax.axis_index("root") * half
    corr_ref[...] = corr_in[...]
    for b in range(residual_ref.shape[1] // size):
        columns = chunk(b, size)
        of_mine = pl.ds(pl.multiple_of(b * size + mine, half), half)
        of_other = pl.ds(pl.multiple_of(b * size + half - mine, half), half)
        for k, kind in enumerate(kinds):
            @pl.when(jnp.logical_and(listed_ref[b] > 0, offset_ref[b] == offset_of(kind)))
            def _():
                solved = jnp.dot(
                    residual_ref[:, of_mine], halves[2 * k][...], preferred_element_type=F32
                ) + jnp.dot(
                    residual_ref[:, of_other], halves[2 * k + 1][...], preferred_element_type=F32
                )
                precond_ref[:, columns] = solved
                corr_ref[...] += correlate(solved, subspace_ref[:, columns])


def last_kernel(size, precond_ref, corr_ref, got_ref, gram_ref, lost_ref, subspace_ref, out_hbm, out_ref, sems):
    corr = corr_ref[...] + got_ref[...].astype(F32)
    coef = corr.astype(BF16)
    again = jnp.dot(coef, gram_ref[...], preferred_element_type=F32)
    coef_2 = corr - again - coef.astype(F32) * lost_ref[0:1, :]
    total = coef.astype(F32) + coef_2
    lead = total.astype(BF16)
    both = jnp.concatenate([lead, (total - lead.astype(F32)).astype(BF16)], axis=0)
    roots = lead.shape[0]
    copies = []
    for b in range(precond_ref.shape[1] // size):
        columns = chunk(b, size)
        basis = subspace_ref[:, columns]
        step = jnp.dot(both, basis, preferred_element_type=F32)
        out_ref[:, columns] = precond_ref[:, columns] - (step[:roots, :] + step[roots:, :])
        copy = pltpu.make_async_copy(out_ref.at[:, columns], out_hbm.at[:, columns], sems.at[b])
        copy.start()
        copies.append(copy)
    for copy in copies:
        copy.wait()


PARAMS = pltpu.CompilerParams(vmem_limit_bytes=24 * 1024 * 1024)


def cost(flops, bytes_accessed):
    return pl.CostEstimate(flops=flops, bytes_accessed=bytes_accessed, transcendentals=0)


def per_device(residual, subspace, inverses, owner_offset, listed):
    roots, columns = residual.shape
    vectors = subspace.shape[0]
    own = inverses[0]
    size = own.shape[0]
    count = columns // size
    core = lax.axis_index("root").astype(jnp.int32)
    half = size // lax.axis_size("root")

    block = vectors // 2
    count_half = 5 * vectors // 16

    def shape(*dims, dtype=BF16):
        return jax.ShapeDtypeStruct(dims, dtype)

    wide = shape(roots, columns, dtype=F32)
    small = shape(roots, vectors, dtype=F32)
    message = shape(count_half + PAD, block)

    def call(kernel, outs, *args, scratch=(), **more):
        return pl.pallas_call(
            kernel,
            out_shape=outs,
            in_specs=[VMEM] * len(args),
            out_specs=jax.tree.map(lambda _: VMEM, outs),
            scratch_shapes=list(scratch),
            compiler_params=PARAMS,
            **more,
        )(*args)

    my_half = lax.dynamic_slice_in_dim(own, core * half, half, 0)
    ahead = permute(my_half, lambda i: i + 2)
    mixed = permute_cores(my_half, lambda i, core: (i ^ core, core))

    subspace, kept, given = pl.pallas_call(
        gram_kernel,
        out_shape=(shape(*subspace.shape), shape(count_half, block, dtype=F32), message),
        in_specs=[HBM],
        out_specs=(VMEM,) * 3,
        scratch_shapes=[pltpu.VMEM((2 * count_half, block), F32), pltpu.SemaphoreType.DMA((4,))],
        cost_estimate=cost(2 * vectors * vectors * columns, 16 * vectors * columns),
        compiler_params=pltpu.CompilerParams(vmem_limit_bytes=46 * 1024 * 1024),
    )(subspace)
    mixed, kept = lax.optimization_barrier((mixed, kept))
    mixed = permute_cores(
        mixed,
        lambda i, core: ((i + 4, 1) if i % 2 else (i, 1)) if core else (i + 1 + 2 * (i % 2), 0),
    )
    gram = call(kept_kernel, message, kept, permute(given, lambda i: i ^ 1))
    ahead, gram = lax.optimization_barrier((ahead, gram))
    swapped = permute(ahead, lambda i: i ^ 1)
    gram = call(add_kernel, message, gram, permute(gram, lambda i: i ^ 2))
    mixed, gram = lax.optimization_barrier((mixed, gram))
    step = 4
    while step < lax.axis_size("tr"):
        gram = call(add_kernel, message, gram, permute(gram, lambda i: i ^ step))
        step *= 2

    precond, corr = pl.pallas_call(
        local_kernel,
        out_shape=(wide, small),
        in_specs=[SMEM, SMEM, VMEM, VMEM, VMEM],
        out_specs=(VMEM,) * 2,
        compiler_params=PARAMS,
    )(owner_offset, listed, residual, subspace, own)

    def fetched(kinds, halves, precond, corr):
        return pl.pallas_call(
            functools.partial(fetched_kernel, kinds),
            out_shape=(wide, small),
            in_specs=[SMEM] * 2 + [VMEM] * (4 + len(halves)),
            out_specs=(VMEM, VMEM),
            input_output_aliases={4 + len(halves): 0},
            cost_estimate=cost(0, 0),
            compiler_params=PARAMS,
        )(owner_offset, listed, residual, subspace, *halves, precond, corr)

    mixed, corr = lax.optimization_barrier((mixed, corr))
    precond, corr = fetched(
        (AHEAD, MIXED, SWAPPED),
        (ahead, other_core(ahead), mixed, other_core(mixed), swapped, other_core(swapped)),
        precond, corr,
    )
    gram_far = permute(gram, lambda i: i ^ 1)
    gram, lost = call(
        assemble_kernel,
        (shape(vectors, vectors), shape(PAD, vectors, dtype=F32)),
        gram, gram_far, other_core(gram), other_core(gram_far),
        scratch=[pltpu.VMEM((2 * count_half, block), F32)],
    )

    step = 1
    while 2 * step < lax.axis_size("tr"):
        corr = corr + permute(corr.astype(BF16), lambda i: i ^ step).astype(F32)
        step *= 2
    got = permute(corr.astype(BF16), lambda i: i ^ step)

    def last(*refs):
        last_kernel(size, *refs)

    return pl.pallas_call(
        last,
        out_shape=wide,
        in_specs=[VMEM] * 6,
        out_specs=HBM,
        scratch_shapes=[pltpu.VMEM((roots, columns), F32), pltpu.SemaphoreType.DMA((count,))],
        compiler_params=PARAMS,
    )(precond, corr, got, gram, lost, subspace)


def solution(mesh):
    return jax.shard_map(
        per_device,
        mesh=mesh,
        in_specs=(
            P("root", ("grp", "tr")),
            P(None, ("grp", "tr")),
            P(("grp", "tr"), None, None),
            P(("grp", "tr")),
            P(("grp", "tr")),
        ),
        out_specs=P("root", ("grp", "tr")),
        check_vma=False,
    )
```

```python
import functools

import jax
import jax.numpy as jnp
from jax import lax
from jax.experimental import pallas as pl
from jax.experimental.pallas import tpu as pltpu
from jax.sharding import PartitionSpec as P

F32 = jnp.float32
BF16 = jnp.bfloat16
VMEM = pl.BlockSpec(memory_space=pltpu.VMEM)
SMEM = pl.BlockSpec(memory_space=pltpu.SMEM)
HBM = pl.BlockSpec(memory_space=pltpu.HBM)
ACROSS = (((1,), (1,)), ((), ()))
AHEAD, MIXED, SWAPPED = range(3)


def permute(block, source):
    n = lax.axis_size("tr")
    return lax.ppermute(block, "tr", [(source(i) % n, i) for i in range(n)])


def permute_cores(block, source):
    n, cores = lax.axis_size("tr"), lax.axis_size("root")
    pairs = []
    for i in range(n):
        for core in range(cores):
            at, of = source(i, core)
            pairs.append((at % n * cores + of, i * cores + core))
    return lax.ppermute(block, ("tr", "root"), pairs)


def other_core(block):
    return lax.ppermute(block, "root", [(0, 1), (1, 0)])


PAD = 16


def diagonal(rows, half):
    quarter = rows[1] // 2
    row = lax.broadcasted_iota(jnp.int32, rows, 0) + half * rows[0]
    column = lax.broadcasted_iota(jnp.int32, rows, 1)
    folded = row - 2 * quarter
    at_end = jnp.logical_and(
        folded >= 0, jnp.logical_or(column == folded, column == folded + quarter + quarter // 2)
    )
    return jnp.logical_or(at_end, jnp.logical_and(row < quarter, column == row))


def encode(message_ref, values, half):
    count = values.shape[0]
    rounded = values.astype(BF16)
    lost = jnp.where(diagonal(values.shape, half), values - rounded.astype(F32), 0.0)
    lost = jnp.sum(lost, axis=0, keepdims=True)
    message_ref[:count, :] = rounded
    message_ref[count:, :] = jnp.broadcast_to(lost, (PAD, values.shape[1])).astype(BF16)


def decode(message_ref, half):
    count = message_ref.shape[0] - PAD
    values = message_ref[:count, :].astype(F32)
    lost = message_ref[count:, :].astype(F32)[0:1, :]
    return values + jnp.where(diagonal(values.shape, half), lost, 0.0)


def gram_kernel(subspace_hbm, subspace_ref, kept_ref, message_ref, gram_ref, sems):
    vectors, columns = subspace_hbm.shape
    core = lax.axis_index("root")
    quarter = vectors // 4
    pieces = sems.shape[0]
    width = columns // pieces
    copies = [
        pltpu.make_async_copy(
            subspace_hbm.at[:, chunk(b, width)], subspace_ref.at[:, chunk(b, width)], sems.at[b]
        )
        for b in range(pieces)
    ]
    for copy in copies:
        copy.start()
    fold = quarter // 2
    for b in range(pieces):
        copies[b].wait()
        span = chunk(b, width)

        def rows(start, count):
            return subspace_ref[pl.ds(pl.multiple_of(start, quarter), count), span]

        near = correlate(rows(2 * core * quarter, 2 * quarter), rows(2 * core * quarter, 2 * quarter))
        far = correlate(rows(core * quarter, quarter), subspace_ref[2 * quarter :, span])
        parts = (
            (0, quarter, slice(None), near[:quarter, :]),
            (quarter, quarter, slice(None), far),
            (2 * quarter, fold, slice(0, quarter), near[quarter : quarter + fold, quarter:]),
            (2 * quarter, fold, slice(quarter, None), near[quarter + fold :, quarter:]),
        )
        for start, count, across, value in parts:
            if b == 0:
                gram_ref[start : start + count, across] = value
            else:
                gram_ref[start : start + count, across] += value
    half = lax.axis_index("tr") % 2
    count = kept_ref.shape[0]
    kept_ref[...] = gram_ref[pl.ds(pl.multiple_of(half * count, count), count), :]
    given = gram_ref[pl.ds(pl.multiple_of((1 - half) * count, count), count), :]
    encode(message_ref, given, 1 - half)


def kept_kernel(kept_ref, got_ref, message_ref):
    half = lax.axis_index("tr") % 2
    encode(message_ref, kept_ref[...] + decode(got_ref, half), half)


def add_kernel(sent_ref, got_ref, message_ref):
    half = lax.axis_index("tr") % 2
    encode(message_ref, decode(sent_ref, half) + decode(got_ref, half), half)


def assemble_kernel(mine_ref, got_ref, mine_other_ref, got_other_ref, gram_ref, lost_ref, packed_ref):
    half = lax.axis_index("tr") % 2
    core = lax.axis_index("root")
    count = mine_ref.shape[0] - PAD
    quarter = mine_ref.shape[1] // 2
    fold = quarter // 2
    for owner, near_ref, far_ref in ((core, mine_ref, got_ref), (1 - core, mine_other_ref, got_other_ref)):
        packed_ref[pl.ds(pl.multiple_of(half * count, count), count), :] = near_ref[:count, :].astype(F32)
        packed_ref[pl.ds(pl.multiple_of((1 - half) * count, count), count), :] = far_ref[:count, :].astype(F32)
        first = pl.ds(pl.multiple_of(2 * owner * quarter, quarter), quarter)
        second = pl.ds(pl.multiple_of(2 * owner * quarter + quarter, quarter), quarter)
        across = packed_ref[:quarter, quarter:]
        gram_ref[first, first] = packed_ref[:quarter, :quarter].astype(BF16)
        gram_ref[first, second] = across.astype(BF16)
        gram_ref[second, first] = across.T.astype(BF16)
        gram_ref[second, second] = jnp.concatenate(
            [packed_ref[2 * quarter :, :quarter], packed_ref[2 * quarter :, quarter:]], axis=0
        ).astype(BF16)
        to = pl.ds(pl.multiple_of(owner * quarter, quarter), quarter)
        outer = packed_ref[quarter : 2 * quarter, :]
        gram_ref[to, 2 * quarter :] = outer.astype(BF16)
        gram_ref[2 * quarter :, to] = outer.T.astype(BF16)
        lost_ref[:, first] = jnp.where(half == 0, near_ref[count:, :quarter], far_ref[count:, :quarter]).astype(F32)
        last = jnp.where(half == 0, far_ref[count:, :], near_ref[count:, :]).astype(F32)
        lane = lax.broadcasted_iota(jnp.int32, (PAD, quarter), 1)
        lost_ref[:, second] = jnp.where(lane < fold, last[:, :quarter], last[:, quarter:])


def correlate(block, basis):
    return lax.dot_general(block.astype(BF16), basis, ACROSS, preferred_element_type=F32)


def chunk(b, size):
    return pl.ds(b * size, size)


def offset_of(kind):
    odd = lax.axis_index("tr") % 2
    return {AHEAD: 2, MIXED: 1 + 2 * odd, SWAPPED: 3 - 2 * odd}[kind]


def local_kernel(offset_ref, listed_ref, residual_ref, subspace_ref, own_ref, precond_ref, corr_ref):
    size = own_ref.shape[0]
    corr_ref[...] = jnp.zeros_like(corr_ref)
    for b in range(residual_ref.shape[1] // size):
        columns = chunk(b, size)
        listed = listed_ref[b] > 0
        own = jnp.logical_and(listed, offset_ref[b] == 0)

        @pl.when(own)
        def _():
            precond_ref[:, columns] = jnp.dot(
                residual_ref[:, columns], own_ref[...], preferred_element_type=F32
            )

        @pl.when(jnp.logical_not(listed))
        def _():
            precond_ref[:, columns] = residual_ref[:, columns].astype(F32)

        @pl.when(jnp.logical_or(own, jnp.logical_not(listed)))
        def _():
            corr_ref[...] += correlate(precond_ref[:, columns], subspace_ref[:, columns])


def fetched_kernel(kinds, offset_ref, listed_ref, residual_ref, subspace_ref, *rest):
    halves, (_, corr_in, precond_ref, corr_ref) = rest[: 2 * len(kinds)], rest[2 * len(kinds) :]
    half = halves[0].shape[0]
    size = 2 * half
    mine = lax.axis_index("root") * half
    corr_ref[...] = corr_in[...]
    for b in range(residual_ref.shape[1] // size):
        columns = chunk(b, size)
        of_mine = pl.ds(pl.multiple_of(b * size + mine, half), half)
        of_other = pl.ds(pl.multiple_of(b * size + half - mine, half), half)
        for k, kind in enumerate(kinds):
            @pl.when(jnp.logical_and(listed_ref[b] > 0, offset_ref[b] == offset_of(kind)))
            def _():
                solved = jnp.dot(
                    residual_ref[:, of_mine], halves[2 * k][...], preferred_element_type=F32
                ) + jnp.dot(
                    residual_ref[:, of_other], halves[2 * k + 1][...], preferred_element_type=F32
                )
                precond_ref[:, columns] = solved
                corr_ref[...] += correlate(solved, subspace_ref[:, columns])


def last_kernel(size, precond_ref, corr_ref, *rest):
    *got_refs, gram_ref, lost_ref, subspace_ref, out_hbm, out_ref, sems = rest
    corr = corr_ref[...]
    for got_ref in got_refs:
        corr += got_ref[...].astype(F32)
    coef = corr.astype(BF16)
    again = jnp.dot(coef, gram_ref[...], preferred_element_type=F32)
    coef_2 = corr - again - coef.astype(F32) * lost_ref[0:1, :]
    total = coef.astype(F32) + coef_2
    lead = total.astype(BF16)
    both = jnp.concatenate([lead, (total - lead.astype(F32)).astype(BF16)], axis=0)
    roots = lead.shape[0]
    copies = []
    for b in range(precond_ref.shape[1] // size):
        columns = chunk(b, size)
        basis = subspace_ref[:, columns]
        step = jnp.dot(both, basis, preferred_element_type=F32)
        out_ref[:, columns] = precond_ref[:, columns] - (step[:roots, :] + step[roots:, :])
        copy = pltpu.make_async_copy(out_ref.at[:, columns], out_hbm.at[:, columns], sems.at[b])
        copy.start()
        copies.append(copy)
    for copy in copies:
        copy.wait()


PARAMS = pltpu.CompilerParams(vmem_limit_bytes=24 * 1024 * 1024)


def cost(flops, bytes_accessed):
    return pl.CostEstimate(flops=flops, bytes_accessed=bytes_accessed, transcendentals=0)


def per_device(residual, subspace, inverses, owner_offset, listed):
    roots, columns = residual.shape
    vectors = subspace.shape[0]
    own = inverses[0]
    size = own.shape[0]
    count = columns // size
    core = lax.axis_index("root").astype(jnp.int32)
    half = size // lax.axis_size("root")

    block = vectors // 2
    count_half = 5 * vectors // 16

    def shape(*dims, dtype=BF16):
        return jax.ShapeDtypeStruct(dims, dtype)

    wide = shape(roots, columns, dtype=F32)
    small = shape(roots, vectors, dtype=F32)
    message = shape(count_half + PAD, block)

    def call(kernel, outs, *args, scratch=(), **more):
        return pl.pallas_call(
            kernel,
            out_shape=outs,
            in_specs=[VMEM] * len(args),
            out_specs=jax.tree.map(lambda _: VMEM, outs),
            scratch_shapes=list(scratch),
            compiler_params=PARAMS,
            **more,
        )(*args)

    my_half = lax.dynamic_slice_in_dim(own, core * half, half, 0)
    ahead = permute(my_half, lambda i: i + 2)
    mixed = permute_cores(my_half, lambda i, core: (i ^ core, core))

    subspace, kept, given = pl.pallas_call(
        gram_kernel,
        out_shape=(shape(*subspace.shape), shape(count_half, block, dtype=F32), message),
        in_specs=[HBM],
        out_specs=(VMEM,) * 3,
        scratch_shapes=[pltpu.VMEM((2 * count_half, block), F32), pltpu.SemaphoreType.DMA((4,))],
        cost_estimate=cost(2 * vectors * vectors * columns, 16 * vectors * columns),
        compiler_params=pltpu.CompilerParams(vmem_limit_bytes=46 * 1024 * 1024),
    )(subspace)
    mixed, kept = lax.optimization_barrier((mixed, kept))
    mixed = permute_cores(
        mixed,
        lambda i, core: ((i + 4, 1) if i % 2 else (i, 1)) if core else (i + 1 + 2 * (i % 2), 0),
    )
    gram = call(kept_kernel, message, kept, permute(given, lambda i: i ^ 1))
    ahead, gram = lax.optimization_barrier((ahead, gram))
    swapped = permute(ahead, lambda i: i ^ 1)
    gram = call(add_kernel, message, gram, permute(gram, lambda i: i ^ 2))
    mixed, gram = lax.optimization_barrier((mixed, gram))
    step = 4
    while step < lax.axis_size("tr"):
        gram = call(add_kernel, message, gram, permute(gram, lambda i: i ^ step))
        step *= 2

    precond, corr = pl.pallas_call(
        local_kernel,
        out_shape=(wide, small),
        in_specs=[SMEM, SMEM, VMEM, VMEM, VMEM],
        out_specs=(VMEM,) * 2,
        compiler_params=PARAMS,
    )(owner_offset, listed, residual, subspace, own)

    def fetched(kinds, halves, precond, corr):
        return pl.pallas_call(
            functools.partial(fetched_kernel, kinds),
            out_shape=(wide, small),
            in_specs=[SMEM] * 2 + [VMEM] * (4 + len(halves)),
            out_specs=(VMEM, VMEM),
            input_output_aliases={4 + len(halves): 0},
            cost_estimate=cost(0, 0),
            compiler_params=PARAMS,
        )(owner_offset, listed, residual, subspace, *halves, precond, corr)

    mixed, corr = lax.optimization_barrier((mixed, corr))
    precond, corr = fetched(
        (AHEAD, MIXED, SWAPPED),
        (ahead, other_core(ahead), mixed, other_core(mixed), swapped, other_core(swapped)),
        precond, corr,
    )
    gram_far = permute(gram, lambda i: i ^ 1)
    gram, lost = call(
        assemble_kernel,
        (shape(vectors, vectors), shape(PAD, vectors, dtype=F32)),
        gram, gram_far, other_core(gram),
        permute_cores(gram, lambda i, core: (i ^ 1, 1 - core)),
        scratch=[pltpu.VMEM((2 * count_half, block), F32)],
    )

    corr = corr + permute(corr.astype(BF16), lambda i: i ^ 1).astype(F32)
    base, got = 2, []
    while base < lax.axis_size("tr"):
        for part in got:
            corr = corr + part.astype(F32)
        steps = [base, 2 * base, 3 * base] if 2 * base < lax.axis_size("tr") else [base]
        sent = corr.astype(BF16)
        got = [permute(sent, lambda i: i ^ step) for step in steps]
        base *= 4

    def last(*refs):
        last_kernel(size, *refs)

    return pl.pallas_call(
        last,
        out_shape=wide,
        in_specs=[VMEM] * (5 + len(got)),
        out_specs=HBM,
        scratch_shapes=[pltpu.VMEM((roots, columns), F32), pltpu.SemaphoreType.DMA((count,))],
        compiler_params=PARAMS,
    )(precond, corr, *got, gram, lost, subspace)


def solution(mesh):
    return jax.shard_map(
        per_device,
        mesh=mesh,
        in_specs=(
            P("root", ("grp", "tr")),
            P(None, ("grp", "tr")),
            P(("grp", "tr"), None, None),
            P(("grp", "tr")),
            P(("grp", "tr")),
        ),
        out_specs=P("root", ("grp", "tr")),
        check_vma=False,
    )
```

```python
import functools

import jax
import jax.numpy as jnp
from jax import lax
from jax.experimental import pallas as pl
from jax.experimental.pallas import tpu as pltpu
from jax.sharding import PartitionSpec as P

F32 = jnp.float32
BF16 = jnp.bfloat16
VMEM = pl.BlockSpec(memory_space=pltpu.VMEM)
SMEM = pl.BlockSpec(memory_space=pltpu.SMEM)
HBM = pl.BlockSpec(memory_space=pltpu.HBM)
ACROSS = (((1,), (1,)), ((), ()))
AHEAD, MIXED, SWAPPED = range(3)


def permute(block, source):
    n = lax.axis_size("tr")
    return lax.ppermute(block, "tr", [(source(i) % n, i) for i in range(n)])


def permute_cores(block, source):
    n, cores = lax.axis_size("tr"), lax.axis_size("root")
    pairs = []
    for i in range(n):
        for core in range(cores):
            at, of = source(i, core)
            pairs.append((at % n * cores + of, i * cores + core))
    return lax.ppermute(block, ("tr", "root"), pairs)


def other_core(block):
    return lax.ppermute(block, "root", [(0, 1), (1, 0)])


PAD = 16


def diagonal(rows, half):
    quarter = rows[1] // 2
    row = lax.broadcasted_iota(jnp.int32, rows, 0) + half * rows[0]
    column = lax.broadcasted_iota(jnp.int32, rows, 1)
    folded = row - 2 * quarter
    at_end = jnp.logical_and(
        folded >= 0, jnp.logical_or(column == folded, column == folded + quarter + quarter // 2)
    )
    return jnp.logical_or(at_end, jnp.logical_and(row < quarter, column == row))


def encode(message_ref, values, half):
    count = values.shape[0]
    rounded = values.astype(BF16)
    lost = jnp.where(diagonal(values.shape, half), values - rounded.astype(F32), 0.0)
    lost = jnp.sum(lost, axis=0, keepdims=True)
    message_ref[:count, :] = rounded
    message_ref[count:, :] = jnp.broadcast_to(lost, (PAD, values.shape[1])).astype(BF16)


def decode(message_ref, half):
    count = message_ref.shape[0] - PAD
    values = message_ref[:count, :].astype(F32)
    lost = message_ref[count:, :].astype(F32)[0:1, :]
    return values + jnp.where(diagonal(values.shape, half), lost, 0.0)


def gram_kernel(subspace_hbm, subspace_ref, kept_ref, message_ref, gram_ref, sems):
    vectors, columns = subspace_hbm.shape
    core = lax.axis_index("root")
    quarter = vectors // 4
    pieces = sems.shape[0]
    width = columns // pieces
    copies = [
        pltpu.make_async_copy(
            subspace_hbm.at[:, chunk(b, width)], subspace_ref.at[:, chunk(b, width)], sems.at[b]
        )
        for b in range(pieces)
    ]
    for copy in copies:
        copy.start()
    fold = quarter // 2
    for b in range(pieces):
        copies[b].wait()
        span = chunk(b, width)

        def rows(start, count):
            return subspace_ref[pl.ds(pl.multiple_of(start, quarter), count), span]

        near = correlate(rows(2 * core * quarter, 2 * quarter), rows(2 * core * quarter, 2 * quarter))
        far = correlate(rows(core * quarter, quarter), subspace_ref[2 * quarter :, span])
        parts = (
            (0, quarter, slice(None), near[:quarter, :]),
            (quarter, quarter, slice(None), far),
            (2 * quarter, fold, slice(0, quarter), near[quarter : quarter + fold, quarter:]),
            (2 * quarter, fold, slice(quarter, None), near[quarter + fold :, quarter:]),
        )
        for start, count, across, value in parts:
            if b == 0:
                gram_ref[start : start + count, across] = value
            else:
                gram_ref[start : start + count, across] += value
    half = lax.axis_index("tr") % 2
    count = kept_ref.shape[0]
    kept_ref[...] = gram_ref[pl.ds(pl.multiple_of(half * count, count), count), :]
    given = gram_ref[pl.ds(pl.multiple_of((1 - half) * count, count), count), :]
    encode(message_ref, given, 1 - half)


def kept_kernel(kept_ref, got_ref, message_ref):
    half = lax.axis_index("tr") % 2
    encode(message_ref, kept_ref[...] + decode(got_ref, half), half)


def add_kernel(sent_ref, got_ref, message_ref):
    half = lax.axis_index("tr") % 2
    encode(message_ref, decode(sent_ref, half) + decode(got_ref, half), half)


def assemble_kernel(mine_ref, got_ref, mine_other_ref, got_other_ref, gram_ref, lost_ref, packed_ref):
    half = lax.axis_index("tr") % 2
    core = lax.axis_index("root")
    count = mine_ref.shape[0] - PAD
    quarter = mine_ref.shape[1] // 2
    fold = quarter // 2
    for owner, near_ref, far_ref in ((core, mine_ref, got_ref), (1 - core, mine_other_ref, got_other_ref)):
        packed_ref[pl.ds(pl.multiple_of(half * count, count), count), :] = near_ref[:count, :].astype(F32)
        packed_ref[pl.ds(pl.multiple_of((1 - half) * count, count), count), :] = far_ref[:count, :].astype(F32)
        first = pl.ds(pl.multiple_of(2 * owner * quarter, quarter), quarter)
        second = pl.ds(pl.multiple_of(2 * owner * quarter + quarter, quarter), quarter)
        across = packed_ref[:quarter, quarter:]
        gram_ref[first, first] = packed_ref[:quarter, :quarter].astype(BF16)
        gram_ref[first, second] = across.astype(BF16)
        gram_ref[second, first] = across.T.astype(BF16)
        gram_ref[second, second] = jnp.concatenate(
            [packed_ref[2 * quarter :, :quarter], packed_ref[2 * quarter :, quarter:]], axis=0
        ).astype(BF16)
        to = pl.ds(pl.multiple_of(owner * quarter, quarter), quarter)
        outer = packed_ref[quarter : 2 * quarter, :]
        gram_ref[to, 2 * quarter :] = outer.astype(BF16)
        gram_ref[2 * quarter :, to] = outer.T.astype(BF16)
        lost_ref[:, first] = jnp.where(half == 0, near_ref[count:, :quarter], far_ref[count:, :quarter]).astype(F32)
        last = jnp.where(half == 0, far_ref[count:, :], near_ref[count:, :]).astype(F32)
        lane = lax.broadcasted_iota(jnp.int32, (PAD, quarter), 1)
        lost_ref[:, second] = jnp.where(lane < fold, last[:, :quarter], last[:, quarter:])


def correlate(block, basis):
    return lax.dot_general(block.astype(BF16), basis, ACROSS, preferred_element_type=F32)


def chunk(b, size):
    return pl.ds(b * size, size)


def offset_of(kind):
    odd = lax.axis_index("tr") % 2
    return {AHEAD: 2, MIXED: 1 + 2 * odd, SWAPPED: 3 - 2 * odd}[kind]


def local_kernel(offset_ref, listed_ref, residual_ref, subspace_ref, own_ref, precond_ref, corr_ref):
    size = own_ref.shape[0]
    corr_ref[...] = jnp.zeros_like(corr_ref)
    for b in range(residual_ref.shape[1] // size):
        columns = chunk(b, size)
        listed = listed_ref[b] > 0
        own = jnp.logical_and(listed, offset_ref[b] == 0)

        @pl.when(own)
        def _():
            precond_ref[:, columns] = jnp.dot(
                residual_ref[:, columns], own_ref[...], preferred_element_type=F32
            )

        @pl.when(jnp.logical_not(listed))
        def _():
            precond_ref[:, columns] = residual_ref[:, columns].astype(F32)

        @pl.when(jnp.logical_or(own, jnp.logical_not(listed)))
        def _():
            corr_ref[...] += correlate(precond_ref[:, columns], subspace_ref[:, columns])


def fetched_kernel(kinds, offset_ref, listed_ref, residual_ref, subspace_ref, *rest):
    halves, (_, corr_in, precond_ref, corr_ref) = rest[: 2 * len(kinds)], rest[2 * len(kinds) :]
    half = halves[0].shape[0]
    size = 2 * half
    mine = lax.axis_index("root") * half
    corr_ref[...] = corr_in[...]
    for b in range(residual_ref.shape[1] // size):
        columns = chunk(b, size)
        of_mine = pl.ds(pl.multiple_of(b * size + mine, half), half)
        of_other = pl.ds(pl.multiple_of(b * size + half - mine, half), half)
        for k, kind in enumerate(kinds):
            @pl.when(jnp.logical_and(listed_ref[b] > 0, offset_ref[b] == offset_of(kind)))
            def _():
                solved = jnp.dot(
                    residual_ref[:, of_mine], halves[2 * k][...], preferred_element_type=F32
                ) + jnp.dot(
                    residual_ref[:, of_other], halves[2 * k + 1][...], preferred_element_type=F32
                )
                precond_ref[:, columns] = solved
                corr_ref[...] += correlate(solved, subspace_ref[:, columns])


def last_kernel(size, precond_ref, corr_ref, *rest):
    *got_refs, gram_ref, lost_ref, subspace_ref, out_hbm, out_ref, sems = rest
    corr = corr_ref[...]
    for got_ref in got_refs:
        corr += got_ref[...].astype(F32)
    coef = corr.astype(BF16)
    again = jnp.dot(coef, gram_ref[...], preferred_element_type=F32)
    coef_2 = corr - again - coef.astype(F32) * lost_ref[0:1, :]
    total = coef.astype(F32) + coef_2
    lead = total.astype(BF16)
    both = jnp.concatenate([lead, (total - lead.astype(F32)).astype(BF16)], axis=0)
    roots = lead.shape[0]
    copies = []
    for b in range(precond_ref.shape[1] // size):
        columns = chunk(b, size)
        basis = subspace_ref[:, columns]
        step = jnp.dot(both, basis, preferred_element_type=F32)
        out_ref[:, columns] = precond_ref[:, columns] - (step[:roots, :] + step[roots:, :])
        copy = pltpu.make_async_copy(out_ref.at[:, columns], out_hbm.at[:, columns], sems.at[b])
        copy.start()
        copies.append(copy)
    for copy in copies:
        copy.wait()


PARAMS = pltpu.CompilerParams(vmem_limit_bytes=24 * 1024 * 1024)


def cost(flops, bytes_accessed):
    return pl.CostEstimate(flops=flops, bytes_accessed=bytes_accessed, transcendentals=0)


def per_device(residual, subspace, inverses, owner_offset, listed):
    roots, columns = residual.shape
    vectors = subspace.shape[0]
    own = inverses[0]
    size = own.shape[0]
    count = columns // size
    core = lax.axis_index("root").astype(jnp.int32)
    half = size // lax.axis_size("root")

    block = vectors // 2
    count_half = 5 * vectors // 16

    def shape(*dims, dtype=BF16):
        return jax.ShapeDtypeStruct(dims, dtype)

    wide = shape(roots, columns, dtype=F32)
    small = shape(roots, vectors, dtype=F32)
    message = shape(count_half + PAD, block)

    def call(kernel, outs, *args, scratch=(), **more):
        return pl.pallas_call(
            kernel,
            out_shape=outs,
            in_specs=[VMEM] * len(args),
            out_specs=jax.tree.map(lambda _: VMEM, outs),
            scratch_shapes=list(scratch),
            compiler_params=PARAMS,
            **more,
        )(*args)

    my_half = lax.dynamic_slice_in_dim(own, core * half, half, 0)
    ahead = permute(my_half, lambda i: i + 2)
    mixed = permute_cores(my_half, lambda i, core: (i ^ core, core))

    subspace, kept, given = pl.pallas_call(
        gram_kernel,
        out_shape=(shape(*subspace.shape), shape(count_half, block, dtype=F32), message),
        in_specs=[HBM],
        out_specs=(VMEM,) * 3,
        scratch_shapes=[pltpu.VMEM((2 * count_half, block), F32), pltpu.SemaphoreType.DMA((4,))],
        cost_estimate=cost(2 * vectors * vectors * columns, 16 * vectors * columns),
        compiler_params=pltpu.CompilerParams(vmem_limit_bytes=46 * 1024 * 1024),
    )(subspace)
    mixed, kept = lax.optimization_barrier((mixed, kept))
    mixed = permute_cores(
        mixed,
        lambda i, core: ((i + 4, 1) if i % 2 else (i, 1)) if core else (i + 1 + 2 * (i % 2), 0),
    )
    gram = call(kept_kernel, message, kept, permute(given, lambda i: i ^ 1))
    ahead, gram = lax.optimization_barrier((ahead, gram))
    swapped = permute(ahead, lambda i: i ^ 1)
    gram = call(add_kernel, message, gram, permute(gram, lambda i: i ^ 2))
    mixed, gram = lax.optimization_barrier((mixed, gram))
    step = 4
    while step < lax.axis_size("tr"):
        gram = call(add_kernel, message, gram, permute(gram, lambda i: i ^ step))
        step *= 2

    precond, corr = pl.pallas_call(
        local_kernel,
        out_shape=(wide, small),
        in_specs=[SMEM, SMEM, VMEM, VMEM, VMEM],
        out_specs=(VMEM,) * 2,
        compiler_params=PARAMS,
    )(owner_offset, listed, residual, subspace, own)

    def fetched(kinds, halves, precond, corr):
        return pl.pallas_call(
            functools.partial(fetched_kernel, kinds),
            out_shape=(wide, small),
            in_specs=[SMEM] * 2 + [VMEM] * (4 + len(halves)),
            out_specs=(VMEM, VMEM),
            input_output_aliases={4 + len(halves): 0},
            cost_estimate=cost(0, 0),
            compiler_params=PARAMS,
        )(owner_offset, listed, residual, subspace, *halves, precond, corr)

    mixed, corr = lax.optimization_barrier((mixed, corr))
    precond, corr = fetched(
        (AHEAD, MIXED, SWAPPED),
        (ahead, other_core(ahead), mixed, other_core(mixed), swapped, other_core(swapped)),
        precond, corr,
    )
    gram_far = permute(gram, lambda i: i ^ 1)
    gram, lost = call(
        assemble_kernel,
        (shape(vectors, vectors), shape(PAD, vectors, dtype=F32)),
        gram, gram_far, other_core(gram),
        permute_cores(gram, lambda i, core: (i ^ 1, 1 - core)),
        scratch=[pltpu.VMEM((2 * count_half, block), F32)],
    )

    groups, base = [[4], [1, 2, 3]], 8
    while base < lax.axis_size("tr"):
        groups.append([base])
        base *= 2
    got = []
    for steps in groups:
        for part in got:
            corr = corr + part.astype(F32)
        sent = corr.astype(BF16)
        got = [permute(sent, lambda i: i ^ step) for step in steps]

    def last(*refs):
        last_kernel(size, *refs)

    return pl.pallas_call(
        last,
        out_shape=wide,
        in_specs=[VMEM] * (5 + len(got)),
        out_specs=HBM,
        scratch_shapes=[pltpu.VMEM((roots, columns), F32), pltpu.SemaphoreType.DMA((count,))],
        compiler_params=PARAMS,
    )(precond, corr, *got, gram, lost, subspace)


def solution(mesh):
    return jax.shard_map(
        per_device,
        mesh=mesh,
        in_specs=(
            P("root", ("grp", "tr")),
            P(None, ("grp", "tr")),
            P(("grp", "tr"), None, None),
            P(("grp", "tr")),
            P(("grp", "tr")),
        ),
        out_specs=P("root", ("grp", "tr")),
        check_vma=False,
    )
```
